256 devices in a mesh: inner: 4 (over x_hi, core), outer: 64 (over y, x_lo, z).
Axes of the slice: x: 4 (x_hi: 2, x_lo: 2; x = x_hi * 2 + x_lo), y: 4, z: 8, core: 2. Of those that a mesh axis runs over, the one named last changes fastest.
Arguments:
- queries: bfloat16 [65536, 512], P(('inner', 'outer')), may hold values from -12 to 12
- keys: bfloat16 [65536, 128], P(('inner', 'outer')), may hold values from -12 to 12
- values: bfloat16 [65536, 128], P(('inner', 'outer')), may hold values from -6 to 6
- out_grad: bfloat16 [65536, 512], P(('inner', 'outer')), may hold values from -6 to 6
- block_place: int32 [512], replicated, may hold values from 0 to 511, each once
Outputs:
- query_grad: bfloat16 [65536, 512], P(('inner', 'outer'))
- key_grad: bfloat16 [65536, 128], P(('inner', 'outer'))
- value_grad: bfloat16 [65536, 128], P(('inner', 'outer'))
The draws below stay inside these ranges and needn't reach their ends.
Inputs may be any that keep to these rules, and one draw needn't show every extreme that they name: `block_place`: every block place appears exactly once.
All inputs are finite; a program needn't handle non-finite values.
Results may differ from the reference program's by a relative error of at most 0.017.
Values may be sent and summed in bfloat16 or wider, within the bound.
A program may use at most 128 MiB of HBM per device.

```python
import math
import jax
import jax.numpy as jnp
from jax import lax

HD = 128
HEADS = 4
TOK_DEV = 256
STEPS = 4
SEQ = 65536
BLOCKS = 512
N_INNER = 4
N_OUTER = 64


def shared_keys(key):
    normals = jax.random.normal(jax.random.fold_in(key, 11), (SEQ, HD), jnp.float32)
    normals = jnp.clip(normals, -6.0, 6.0)
    return normals


def draw_keys(key, part):
    return shared_keys(key).astype(jnp.bfloat16)


def draw_queries(key, part):
    normals = jnp.clip(jax.random.normal(jax.random.fold_in(key, 12), (SEQ, HEADS, HD), jnp.float32), -6.0, 6.0)
    return normals.reshape(SEQ, HEADS * HD).astype(jnp.bfloat16)


def shard_levels(key, dims, cuts, least, largest):
    factor_of, own = 1.0, jax.random.fold_in(key, 6)
    for axis_at, blocks in cuts:
        heights = jnp.exp(jax.random.uniform(jax.random.fold_in(own, axis_at), (blocks,), jnp.float32, least / len(cuts), largest / len(cuts)))
        factor_of = factor_of * jnp.repeat(heights, dims[axis_at] // blocks).reshape([-1 if axis == axis_at else 1 for axis in range(len(dims))])
    return factor_of


def centred(rng, extent, spread, most, cuts=(), held_as=jnp.bfloat16):
    drawn = jax.random.normal(rng, extent, jnp.float32) * spread
    if len(cuts) > 0:
        drawn = shard_levels(rng, extent, cuts, -0.22, 0.18) * drawn
    return jnp.clip(drawn, min=-most, max=most).astype(held_as)


def setup_inputs(seed: int = 0) -> dict:
    key_list = jax.random.split(jax.random.key(seed), 6)
    queries = draw_queries(jax.random.fold_in(key_list[5], 71), 0)
    keys = draw_keys(jax.random.fold_in(key_list[5], 71), 0)
    values = centred(key_list[2], (SEQ, HD), 1.0, 6.0, ((0, 256),))
    out_grad = centred(key_list[3], (SEQ, HEADS * HD), 1.0, 6.0, ((0, 256),))
    block_place = jax.random.permutation(key_list[4], BLOCKS).astype(jnp.int32)
    return dict(queries=queries, keys=keys, values=values, out_grad=out_grad, block_place=block_place)


def reference(queries, keys, values, out_grad, block_place):
    all_rows = keys.shape[0]
    head_size = keys.shape[1]
    row_count = TOK_DEV
    block_len = row_count // 2
    group_rows = N_INNER * row_count
    score_scale = 1.0 / math.sqrt(head_size)
    offsets = jnp.arange(block_len, dtype=jnp.int32)
    place = (block_place.astype(jnp.int32)[:, None] * block_len + offsets[None, :]).reshape(all_rows)
    place_grid = place.reshape(N_INNER, N_OUTER, row_count)
    key_grid = keys.astype(jnp.float32).reshape(N_INNER, N_OUTER, row_count, head_size)
    value_grid = values.astype(jnp.float32).reshape(N_INNER, N_OUTER, row_count, head_size)
    query_grid = queries.astype(jnp.float32).reshape(N_INNER, N_OUTER, row_count, HEADS, head_size)
    grad_grid = out_grad.astype(jnp.float32).reshape(N_INNER, N_OUTER, row_count, HEADS, head_size)

    def window(grid, group):
        pieces = []
        for step in range(STEPS):
            source = ((group - step) % N_OUTER).astype(jnp.int32)
            pieces.append(lax.dynamic_index_in_dim(grid, source, 1, False))
        whole = jnp.stack(pieces, axis=0)
        return whole.reshape((STEPS * group_rows,) + grid.shape[3:])

    def one_device(state, device):
        key_acc, value_acc = state
        inner_i = (device // N_OUTER).astype(jnp.int32)
        group = (device % N_OUTER).astype(jnp.int32)
        query_f = lax.dynamic_index_in_dim(lax.dynamic_index_in_dim(query_grid, inner_i, 0, False), group, 0, False)
        grad_f = lax.dynamic_index_in_dim(lax.dynamic_index_in_dim(grad_grid, inner_i, 0, False), group, 0, False)
        query_place = lax.dynamic_index_in_dim(lax.dynamic_index_in_dim(place_grid, inner_i, 0, False), group, 0, False)
        keys_f = window(key_grid, group)
        values_f = window(value_grid, group)
        key_place = window(place_grid, group)
        scores = jnp.einsum('thd,kd->thk', query_f, keys_f) * score_scale
        allowed = key_place[None, None, :] <= query_place[:, None, None]
        scores = jnp.where(allowed, scores, -1e+30)
        row_max = lax.optimization_barrier(jnp.max(scores, axis=-1))
        log_total = row_max + jnp.log(lax.optimization_barrier(jnp.sum(jnp.where(allowed, jnp.exp(scores - row_max[..., None]), 0.0), axis=-1)))
        probs = jnp.where(allowed, jnp.exp(scores - log_total[..., None]), 0.0)
        probs_low = probs.astype(jnp.bfloat16)
        probs_low_f = probs_low.astype(jnp.float32)
        attended = jnp.einsum('thk,kd->thd', probs_low_f, values_f)
        row_dot = lax.optimization_barrier(jnp.sum(grad_f * attended, axis=-1))
        grad_probs = jnp.einsum('thd,kd->thk', grad_f, values_f)
        grad_scores = (probs * (grad_probs - row_dot[..., None])).astype(jnp.bfloat16)
        grad_scores_f = grad_scores.astype(jnp.float32)
        query_grad = (jnp.einsum('thk,kd->thd', grad_scores_f, keys_f) * score_scale).astype(jnp.bfloat16)
        key_part = (jnp.einsum('thk,thd->kd', grad_scores_f, query_f) * score_scale).reshape(STEPS, N_INNER, 1, row_count, head_size)
        value_part = jnp.einsum('thk,thd->kd', probs_low_f, grad_f).reshape(STEPS, N_INNER, 1, row_count, head_size)
        zero_index = jnp.zeros((), jnp.int32)
        for step in range(STEPS):
            source = ((group - step) % N_OUTER).astype(jnp.int32)
            corner = (zero_index, source, zero_index, zero_index)
            size = (N_INNER, 1, row_count, head_size)
            key_acc = lax.dynamic_update_slice(key_acc, lax.dynamic_slice(key_acc, corner, size) + key_part[step], corner)
            value_acc = lax.dynamic_update_slice(value_acc, lax.dynamic_slice(value_acc, corner, size) + value_part[step], corner)
        return ((key_acc, value_acc), query_grad.reshape(row_count, HEADS * head_size))
    zero_grid = jnp.zeros((N_INNER, N_OUTER, row_count, head_size), jnp.float32)
    devices = jnp.arange(N_INNER * N_OUTER, dtype=jnp.int32)
    (key_acc, value_acc), query_parts = lax.scan(one_device, (zero_grid, zero_grid), devices)
    query_grad = query_parts.reshape(all_rows, HEADS * head_size)
    return (query_grad, key_acc.reshape(all_rows, head_size).astype(jnp.bfloat16), value_acc.reshape(all_rows, head_size).astype(jnp.bfloat16))
```

```python
import functools
import math

import jax
import jax.numpy as jnp
from jax import lax
from jax.experimental import pallas as pl
from jax.experimental.pallas import tpu as pltpu
from jax.sharding import PartitionSpec as P

STEPS = 4
F32, BF16 = jnp.float32, jnp.bfloat16
MESH = pl.DeviceIdType.MESH
LOW = -1e30


def dot(a, b, over=(1, 0)):
    dims = (((over[0],), (over[1],)), ((), ()))
    return lax.dot_general(a, b, dims, preferred_element_type=F32)


def kernel(
    inner_size, outer_size, tokens, size, heads,
    place_ref, q_hbm, k_hbm, v_hbm, g_hbm, dq_hbm, dk_hbm, dv_hbm,
    kv, q_rows, g_rows, q_cols, g_cols, probs, grads, maxes, run_max, run_sum, run_dot, dq_cols,
    near, far, core_out, core_in, pair_out, pair_in, ring_out, ring_in, dq_rows,
    load_sem, store_sem,
    ring_s, ring_r, core_s, core_r, pair_s, pair_r,
    back_ring_s, back_ring_r, back_core_s, back_core_r, back_pair_s, back_pair_r,
):
    inner, outer = lax.axis_index("inner"), lax.axis_index("outer")
    other_core = inner + 1 - 2 * (inner % 2)
    other_pair = (inner + 2) % inner_size
    other_both = inner_size - 1 - inner
    after = (outer + 1) % outer_size
    before = (outer + outer_size - 1) % outer_size
    columns = (inner, other_core, other_pair, other_both)
    rows = heads * tokens
    block = tokens // 2
    scale = 1.0 / math.sqrt(size)
    scale2 = scale * math.log2(math.e)

    loads = [
        pltpu.make_async_copy(k_hbm, kv.at[0, 0], load_sem.at[0]),
        pltpu.make_async_copy(v_hbm, kv.at[0, 1], load_sem.at[1]),
    ]
    for h in range(heads):
        there = pl.ds(h * tokens, tokens)
        cut = pl.ds(h * size, size)
        loads.append(pltpu.make_async_copy(q_hbm.at[:, cut], q_rows.at[there], load_sem.at[2 + 2 * h]))
        loads.append(pltpu.make_async_copy(g_hbm.at[:, cut], g_rows.at[there], load_sem.at[3 + 2 * h]))
    for load in loads:
        load.start()

    partners = ((other_core, outer), (other_pair, outer), (inner, after), (inner, before))
    barrier = pltpu.get_barrier_semaphore()
    for partner in partners:
        pl.semaphore_signal(barrier, inc=1, device_id=partner, device_id_type=MESH)
    pl.semaphore_wait(barrier, len(partners))

    def remote(src, dst, send, recv, to):
        return pltpu.make_async_remote_copy(
            src_ref=src, dst_ref=dst, send_sem=send, recv_sem=recv, device_id=to, device_id_type=MESH
        )

    def ring(s):
        return remote(kv.at[4 * s], kv.at[4 * s + 4], ring_s.at[s], ring_r.at[s], (inner, after))

    def core(s, j):
        return remote(
            kv.at[4 * s + 2 * j], kv.at[4 * s + 2 * j + 1], core_s.at[2 * s + j], core_r.at[2 * s + j],
            (other_core, outer),
        )

    def pair(s):
        return remote(kv.at[4 * s], kv.at[4 * s + 2], pair_s.at[s], pair_r.at[s], (other_pair, outer))

    loads[0].wait()
    loads[1].wait()
    ring(0).start()
    pair(0).start()
    core(0, 0).start()

    lane = lax.broadcasted_iota(jnp.int32, (1, rows), 1)
    own_block = 2 * (inner * outer_size + outer)
    q_place = jnp.where((lane // block) % 2 == 0, place_ref[own_block], place_ref[own_block + 1])
    for load in loads[2:]:
        load.wait()
    for h in range(heads):
        there = pl.ds(h * tokens, tokens)
        q_cols[:, there] = q_rows[there, :].T
        g_cols[:, there] = g_rows[there, :].T

    def key_block(s, j):
        return 2 * (columns[j] * outer_size + (outer + outer_size - s) % outer_size)

    def forward(chunks, first=False):
        ids = [4 * s + j for s, j in chunks]
        keys = jnp.concatenate([kv[c, 0] for c in ids], axis=0)
        values = jnp.concatenate([kv[c, 1] for c in ids], axis=0)
        places = [place_ref[key_block(s, j) + b] for s, j in chunks for b in range(2)]
        for h in range(heads):
            at = slice(h * tokens, (h + 1) * tokens)
            place = q_place[:, at]
            bias = [
                jnp.broadcast_to(jnp.where(p <= place, 0.0, LOW).astype(F32), (block, tokens)) for p in places
            ]
            if first:
                row = lax.broadcasted_iota(jnp.int32, (block, tokens), 0)
                col = lax.broadcasted_iota(jnp.int32, (block, tokens), 1) % block
                for b in range(2):
                    ok = places[b] * block + row <= place * block + col
                    bias[b] = jnp.where(ok, 0.0, LOW).astype(F32)
            scores = dot(keys, q_cols[:, at]) * scale2 + jnp.concatenate(bias, axis=0)
            grad_probs = dot(values, g_cols[:, at])
            new_max = jnp.max(scores, axis=0, keepdims=True)
            if not first:
                old_max = run_max[:, at]
                new_max = jnp.maximum(old_max, new_max)
                fade = jnp.exp2(old_max - new_max)
            weights = jnp.exp2(scores - new_max)
            part_sum = jnp.sum(weights, axis=0, keepdims=True)
            part_dot = jnp.sum(weights * grad_probs, axis=0, keepdims=True)
            if not first:
                part_sum += run_sum[:, at] * fade
                part_dot += run_dot[:, at] * fade
            run_sum[:, at] = part_sum
            run_dot[:, at] = part_dot
            run_max[:, at] = new_max
            for n, c in enumerate(ids):
                mine = slice(n * tokens, (n + 1) * tokens)
                probs[c, :, at] = weights[mine].astype(BF16)
                grads[c, :, at] = grad_probs[mine]
                maxes[c, :, at] = new_max

    core(0, 0).wait_recv()
    forward(((0, 0), (0, 1)), first=True)

    def arrive(s, _):
        ring(s - 1).wait_recv()

        @pl.when(s < STEPS - 1)
        def _():
            ring(s).start()

        pair(s).start()
        core(s, 0).start()
        pair(s - 1).wait_recv()
        core(s - 1, 1).start()
        forward(((s, 0), (s - 1, 2)))
        core(s, 0).wait_recv()
        core(s - 1, 1).wait_recv()
        forward(((s, 1), (s - 1, 3)))
        return 0

    lax.fori_loop(1, STEPS, arrive, 0)
    last = STEPS - 1
    pair(last).wait_recv()
    core(last, 1).start()
    core(last, 1).wait_recv()
    forward(((last, 2), (last, 3)))

    inverse = 1.0 / run_sum[...]
    run_sum[...] = inverse
    run_dot[...] = run_dot[...] * inverse
    dq_cols[...] = jnp.zeros_like(dq_cols)

    def backward(ids):
        keys = jnp.concatenate([kv[c, 0] for c in ids], axis=0)
        dk = jnp.zeros((len(ids) * tokens, size), F32)
        dv = jnp.zeros((len(ids) * tokens, size), F32)
        factors = [jnp.exp2(maxes[c] - run_max[...]) * run_sum[...] for c in ids]
        for h in range(heads):
            at = slice(h * tokens, (h + 1) * tokens)
            low, slopes = [], []
            for c, factor in zip(ids, factors):
                weights = probs[c, :, at].astype(F32) * factor[:, at]
                low.append(weights.astype(BF16))
                slopes.append((weights * (grads[c, :, at] - run_dot[:, at])).astype(BF16))
            low = jnp.concatenate(low, axis=0)
            slopes = jnp.concatenate(slopes, axis=0)
            dv += dot(low, g_rows[at, :])
            dk += dot(slopes, q_rows[at, :])
            dq_cols[:, at] += dot(keys, slopes, (0, 0))
        dk = dk * scale
        return [
            (dk[n * tokens : (n + 1) * tokens], dv[n * tokens : (n + 1) * tokens]) for n in range(len(ids))
        ]

    def back_core(s, j):
        n = 2 * s + j
        return remote(core_out.at[n], core_in.at[n], back_core_s.at[n], back_core_r.at[n], (other_core, outer))

    def back_pair(s):
        return remote(pair_out.at[s], pair_in.at[s], back_pair_s.at[s], back_pair_r.at[s], (other_pair, outer))

    def back_ring(s):
        return remote(ring_out.at[s], ring_in.at[s - 1], back_ring_s.at[s], back_ring_r.at[s - 1], (inner, before))

    def total(s):
        back_core(s, 0).wait_recv()
        back_pair(s).wait_recv()
        return near[s] + core_in[2 * s].astype(F32) + pair_in[s].astype(F32)

    def arrived(s):
        return pltpu.make_async_remote_copy(
            src_ref=ring_out.at[s], dst_ref=ring_in.at[s], send_sem=back_ring_s.at[s], recv_sem=back_ring_r.at[s],
            device_id=(inner, before), device_id_type=MESH,
        )

    def settle(s):
        whole = total(s)
        if s < STEPS - 1:
            arrived(s).wait_recv()
            whole = whole + ring_in[s].astype(F32)
        ring_out[s] = whole.astype(BF16)
        if s > 0:
            back_ring(s).start()

    def leave(n, _):
        s = STEPS - 1 - n
        pairs = backward((4 * s + 3, 4 * s + 2))
        core_out[2 * s + 1, 0] = pairs[0][0].astype(BF16)
        core_out[2 * s + 1, 1] = pairs[0][1].astype(BF16)
        back_core(s, 1).start()
        far[0] = pairs[1][0]
        far[1] = pairs[1][1]
        pairs = backward((4 * s + 1, 4 * s))
        core_out[2 * s, 0] = pairs[0][0].astype(BF16)
        core_out[2 * s, 1] = pairs[0][1].astype(BF16)
        back_core(s, 0).start()
        near[s, 0] = pairs[1][0]
        near[s, 1] = pairs[1][1]
        back_core(s, 1).wait_recv()
        pair_out[s] = (far[...] + core_in[2 * s + 1].astype(F32)).astype(BF16)
        back_pair(s).start()

        @pl.when(n == 2)
        def _():
            settle(STEPS - 1)

        return 0

    lax.fori_loop(0, STEPS, leave, 0)

    for h in range(heads):
        part = dq_cols[:, h * tokens : (h + 1) * tokens] * scale
        dq_rows[:, h * size : (h + 1) * size] = part.T.astype(BF16)
    store_dq = pltpu.make_async_copy(dq_rows, dq_hbm, store_sem.at[0])
    store_dq.start()
    for s in reversed(range(STEPS - 1)):
        settle(s)
    store_dk = pltpu.make_async_copy(ring_out.at[0, 0], dk_hbm, store_sem.at[1])
    store_dv = pltpu.make_async_copy(ring_out.at[0, 1], dv_hbm, store_sem.at[2])
    store_dk.start()
    store_dv.start()
    for s in range(STEPS):
        pair(s).wait_send()
        back_pair(s).wait_send()
        for j in range(2):
            core(s, j).wait_send()
            back_core(s, j).wait_send()
        if s < STEPS - 1:
            ring(s).wait_send()
            back_ring(s + 1).wait_send()
    store_dq.wait()
    store_dk.wait()
    store_dv.wait()


def per_device(queries, keys, values, out_grad, block_place):
    tokens, size = keys.shape
    heads = queries.shape[1] // size
    rows = heads * tokens
    chunks = 4 * STEPS
    dma = pltpu.SemaphoreType.DMA
    hbm = pl.BlockSpec(memory_space=pl.ANY)
    kept = lambda *shape: pltpu.VMEM(shape, F32)
    low = lambda *shape: pltpu.VMEM(shape, BF16)
    body = functools.partial(
        kernel, lax.axis_size("inner"), lax.axis_size("outer"), tokens, size, heads
    )
    return pl.pallas_call(
        body,
        out_shape=(
            jax.ShapeDtypeStruct(queries.shape, BF16),
            jax.ShapeDtypeStruct(keys.shape, BF16),
            jax.ShapeDtypeStruct(values.shape, BF16),
        ),
        in_specs=[pl.BlockSpec(memory_space=pltpu.SMEM), hbm, hbm, hbm, hbm],
        out_specs=(hbm, hbm, hbm),
        scratch_shapes=[
            low(chunks, 2, tokens, size),
            low(rows, size), low(rows, size), low(size, rows), low(size, rows),
            low(chunks, tokens, rows), kept(chunks, tokens, rows), kept(chunks, 1, rows),
            kept(1, rows), kept(1, rows), kept(1, rows), kept(size, rows),
            kept(STEPS, 2, tokens, size), kept(2, tokens, size),
            low(2 * STEPS, 2, tokens, size), low(2 * STEPS, 2, tokens, size),
            low(STEPS, 2, tokens, size), low(STEPS, 2, tokens, size),
            low(STEPS, 2, tokens, size), low(STEPS, 2, tokens, size),
            low(tokens, heads * size),
            dma((2 + 2 * heads,)), dma((3,)),
            dma((STEPS,)), dma((STEPS,)), dma((2 * STEPS,)), dma((2 * STEPS,)), dma((STEPS,)), dma((STEPS,)),
            dma((STEPS,)), dma((STEPS,)), dma((2 * STEPS,)), dma((2 * STEPS,)), dma((STEPS,)), dma((STEPS,)),
        ],
        compiler_params=pltpu.CompilerParams(
            collective_id=0, has_side_effects=True, vmem_limit_bytes=58 * 2**20
        ),
        cost_estimate=pl.CostEstimate(
            flops=10 * rows * chunks * tokens * size, bytes_accessed=6 * tokens * size * (heads + 1), transcendentals=rows * chunks * tokens
        ),
        name="attention_backward",
    )(block_place, queries, keys, values, out_grad)


def solution(mesh):
    placed = P(("inner", "outer"), None)
    return jax.shard_map(
        per_device,
        mesh=mesh,
        in_specs=(placed, placed, placed, placed, P()),
        out_specs=(placed, placed, placed),
        check_vma=False,
    )
```

```python
import functools
import math

import jax
import jax.numpy as jnp
from jax import lax
from jax.experimental import pallas as pl
from jax.experimental.pallas import tpu as pltpu
from jax.sharding import PartitionSpec as P

STEPS = 4
LINE = 8
DIAG = False
SWAP = True
F32, BF16 = jnp.float32, jnp.bfloat16
MESH = pl.DeviceIdType.MESH
LOW = -1e30


def dot(a, b, over=(1, 0)):
    dims = (((over[0],), (over[1],)), ((), ()))
    return lax.dot_general(a, b, dims, preferred_element_type=F32)


def kernel(
    inner_size, outer_size, tokens, size, heads,
    place_ref, q_hbm, k_hbm, v_hbm, g_hbm, dq_hbm, dk_hbm, dv_hbm,
    kv, q_nat, g_nat, q_cols, g_cols, probs, grads, maxes, stats, stats_in, dq_cols, dq_in,
    near, pair_out, pair_in, ring_out, ring_in, diag_in, dq_rows,
    load_sem, store_sem, q_s, q_r, stats_s, stats_r, dq_s, dq_r,
    ring_s, ring_r, pair_s, pair_r, diag_s, diag_r,
    back_ring_s, back_ring_r, back_pair_s, back_pair_r, back_diag_s, back_diag_r,
):
    inner, outer = lax.axis_index("inner"), lax.axis_index("outer")
    core, depth = inner % 2, outer % LINE
    other_core = inner + 1 - 2 * core
    other_pair = (inner + 2) % inner_size
    crossing = core if SWAP else 0 * core
    after_side = (inner + 2 * crossing * (depth // (LINE - 1))) % inner_size
    before_side = (inner + 2 * crossing * ((LINE - 1 - depth) // (LINE - 1))) % inner_size
    after = (after_side, (outer + 1) % outer_size)
    before = (before_side, (outer + outer_size - 1) % outer_size)
    after_pair = ((after_side + 2) % inner_size, after[1])
    before_pair = ((before_side + 2) % inner_size, before[1])
    mate = (other_core, outer)
    pair = (other_pair, outer)
    own_rows = heads * tokens
    rows = 2 * own_rows
    block = tokens // 2
    scale = 1.0 / math.sqrt(size)
    scale2 = scale * math.log2(math.e)

    loads = [
        pltpu.make_async_copy(src, dst, load_sem.at[n])
        for n, (src, dst) in enumerate(
            ((k_hbm, kv.at[0, 0]), (v_hbm, kv.at[0, 1]), (q_hbm, q_nat.at[0]), (g_hbm, g_nat.at[0]))
        )
    ]
    for load in loads:
        load.start()

    partners = [mate, pair, after, before] + ([after_pair, before_pair] if DIAG else [])
    barrier = pltpu.get_barrier_semaphore()
    for partner in partners:
        pl.semaphore_signal(barrier, inc=1, device_id=partner, device_id_type=MESH)
    pl.semaphore_wait(barrier, len(partners))

    def remote(src, dst, send, recv, to):
        return pltpu.make_async_remote_copy(
            src_ref=src, dst_ref=dst, send_sem=send, recv_sem=recv, device_id=to, device_id_type=MESH
        )

    def ring(s, p):
        return remote(kv.at[2 * s, p], kv.at[2 * s + 2, p], ring_s.at[2 * s + p], ring_r.at[2 * s + p], after)

    def side(s, p):
        return remote(kv.at[2 * s, p], kv.at[2 * s + 1, p], pair_s.at[2 * s + p], pair_r.at[2 * s + p], pair)

    def diag(p):
        last = 2 * STEPS
        return remote(kv.at[last - 4, p], kv.at[last - 1, p], diag_s.at[p], diag_r.at[p], after_pair)

    q_over = remote(q_hbm, q_nat.at[1], q_s.at[0], q_r.at[0], mate)
    g_over = remote(g_hbm, g_nat.at[1], q_s.at[1], q_r.at[1], mate)
    for p in range(2):
        loads[p].wait()
        ring(0, p).start()
        side(0, p).start()
    q_over.start()
    g_over.start()

    lane = lax.broadcasted_iota(jnp.int32, (1, own_rows), 1)

    def row_places(side_inner):
        first_block = 2 * (side_inner * outer_size + outer)
        return jnp.where((lane // block) % 2 == 0, place_ref[first_block], place_ref[first_block + 1])

    q_place = jnp.concatenate([row_places(inner), row_places(other_core)], axis=1)

    def turn(n):
        for h in range(heads):
            there = pl.ds(n * own_rows + h * tokens, tokens)
            q_cols[:, there] = q_nat[n, :, h * size : (h + 1) * size].T
            g_cols[:, there] = g_nat[n, :, h * size : (h + 1) * size].T

    loads[2].wait()
    loads[3].wait()
    turn(0)
    q_over.wait_recv()
    g_over.wait_recv()
    turn(1)

    def key_block(s, j):
        crossed = jnp.where(depth < s, crossing, 0)
        column = (inner + 2 * crossed + 2 * j) % inner_size
        return 2 * (column * outer_size + (outer + outer_size - s) % outer_size)

    def forward(s, j, first=False):
        c = 2 * s + j
        keys, values = kv[c, 0], kv[c, 1]
        places = [place_ref[key_block(s, j) + b] for b in range(2)]
        for t in range(rows // tokens):
            at = slice(t * tokens, (t + 1) * tokens)
            place = q_place[:, at]
            bias = [jnp.broadcast_to(jnp.where(p <= place, 0.0, LOW).astype(F32), (block, tokens)) for p in places]
            if first and t < heads:
                row = lax.broadcasted_iota(jnp.int32, (block, tokens), 0)
                col = lax.broadcasted_iota(jnp.int32, (block, tokens), 1) % block
                for b in range(2):
                    ok = places[b] * block + row <= place * block + col
                    bias[b] = jnp.where(ok, 0.0, LOW).astype(F32)
            scores = dot(keys, q_cols[:, at]) * scale2 + jnp.concatenate(bias, axis=0)
            grad_probs = dot(values, g_cols[:, at])
            new_max = jnp.max(scores, axis=0, keepdims=True)
            if not first:
                old_max = stats[0:1, at]
                new_max = jnp.maximum(old_max, new_max)
                fade = jnp.exp2(old_max - new_max)
            weights = jnp.exp2(scores - new_max)
            part_sum = jnp.sum(weights, axis=0, keepdims=True)
            part_dot = jnp.sum(weights * grad_probs, axis=0, keepdims=True)
            if not first:
                part_sum += stats[1:2, at] * fade
                part_dot += stats[2:3, at] * fade
            stats[0:1, at] = new_max
            stats[1:2, at] = part_sum
            stats[2:3, at] = part_dot
            probs[c, :, at] = weights.astype(BF16)
            grads[c, :, at] = grad_probs
            maxes[c, :, at] = new_max

    forward(0, 0, first=True)

    def arrive(s, _):
        for p in range(2):
            ring(s - 1, p).wait_recv()

            @pl.when(s < STEPS - 1)
            def _():
                ring(s, p).start()
                side(s, p).start()
                if DIAG:
                    @pl.when(s == STEPS - 2)
                    def _():
                        diag(p).start()
            if not DIAG:
                @pl.when(s == STEPS - 1)
                def _():
                    side(s, p).start()

        forward(s, 0)
        side(s - 1, 0).wait_recv()
        side(s - 1, 1).wait_recv()
        forward(s - 1, 1)
        return 0

    lax.fori_loop(1, STEPS, arrive, 0)
    last = STEPS - 1
    for p in range(2):
        (diag(p) if DIAG else side(last, p)).wait_recv()
    forward(last, 1)

    def swap_stats(n):
        here = pl.ds(n * own_rows, own_rows)
        there = pl.ds((1 - n) * own_rows, own_rows)
        return remote(stats.at[:, here], stats_in.at[:, there], stats_s.at[n], stats_r.at[n], mate)

    for n in range(2):
        swap_stats(n).start()
    dq_cols[...] = jnp.zeros_like(dq_cols)
    for n in range(2):
        swap_stats(n).wait()
    top = jnp.maximum(stats[0:1, :], stats_in[0:1, :])
    here, there = jnp.exp2(stats[0:1, :] - top), jnp.exp2(stats_in[0:1, :] - top)
    inverse = 1.0 / (stats[1:2, :] * here + stats_in[1:2, :] * there)
    mean = (stats[2:3, :] * here + stats_in[2:3, :] * there) * inverse
    stats[0:1, :] = top
    stats[1:2, :] = inverse
    stats[2:3, :] = mean

    def backward(c):
        keys = kv[c, 0]
        dk = jnp.zeros((tokens, size), F32)
        dv = jnp.zeros((tokens, size), F32)
        factor = jnp.exp2(maxes[c] - stats[0:1, :]) * stats[1:2, :]
        for t in range(rows // tokens):
            at = slice(t * tokens, (t + 1) * tokens)
            n, h = t // heads, t % heads
            cut = slice(h * size, (h + 1) * size)
            weights = probs[c, :, at].astype(F32) * factor[:, at]
            slopes = (weights * (grads[c, :, at] - stats[2:3, at])).astype(BF16)
            dv += dot(weights.astype(BF16), g_nat[n, :, cut])
            dk += dot(slopes, q_nat[n, :, cut])
            dq_cols[:, at] += dot(keys, slopes, (0, 0))
        return dk * scale, dv

    def back_side(s):
        return remote(pair_out.at[s], pair_in.at[s], back_pair_s.at[s], back_pair_r.at[s], pair)

    def back_diag():
        return remote(pair_out.at[last], diag_in, back_diag_s.at[0], back_diag_r.at[0], before_pair)

    def back_ring(s, p):
        n = 2 * s + p
        return remote(ring_out.at[s, p], ring_in.at[s - 1, p], back_ring_s.at[n], back_ring_r.at[n - 2], before)

    def arrived(s, p):
        n = 2 * s + p
        return remote(ring_out.at[s, p], ring_in.at[s, p], back_ring_s.at[n], back_ring_r.at[n], before)

    def settle(s):
        direct = DIAG and s == last
        if not direct:
            back_side(s).wait_recv()
        if DIAG and s == last - 1:
            back_diag().wait_recv()
        for p in range(2):
            whole = near[s, p]
            if not direct:
                whole = whole + pair_in[s, p].astype(F32)
            if DIAG and s == last - 1:
                whole = whole + diag_in[p].astype(F32)
            if s < last:
                arrived(s, p).wait_recv()
                whole = whole + ring_in[s, p].astype(F32)
            ring_out[s, p] = whole.astype(BF16)
            if s > 0:
                back_ring(s, p).start()

    def leave(n, _):
        s = last - n
        dk, dv = backward(2 * s + 1)
        pair_out[s, 0] = dk.astype(BF16)
        pair_out[s, 1] = dv.astype(BF16)
        if DIAG:
            @pl.when(n == 0)
            def _():
                back_diag().start()

            @pl.when(n > 0)
            def _():
                back_side(s).start()
        else:
            back_side(s).start()
        dk, dv = backward(2 * s)
        near[s, 0] = dk
        near[s, 1] = dv

        @pl.when(n == (0 if DIAG else 2))
        def _():
            settle(last)

        return 0

    lax.fori_loop(0, STEPS, leave, 0)

    dq_over = remote(dq_cols.at[:, pl.ds(own_rows, own_rows)], dq_in, dq_s.at[0], dq_r.at[0], mate)
    dq_over.start()
    settle(last - 1)
    dq_over.wait_recv()
    for h in range(heads):
        there = slice(h * tokens, (h + 1) * tokens)
        part = (dq_cols[:, there] + dq_in[:, there]) * scale
        dq_rows[:, h * size : (h + 1) * size] = part.T.astype(BF16)
    store_dq = pltpu.make_async_copy(dq_rows, dq_hbm, store_sem.at[0])
    store_dq.start()
    for s in reversed(range(last - 1)):
        settle(s)
    store_dk = pltpu.make_async_copy(ring_out.at[0, 0], dk_hbm, store_sem.at[1])
    store_dv = pltpu.make_async_copy(ring_out.at[0, 1], dv_hbm, store_sem.at[2])
    store_dk.start()
    store_dv.start()
    q_over.wait_send()
    g_over.wait_send()
    dq_over.wait_send()
    for s in range(STEPS):
        for p in range(2):
            if s < last:
                ring(s, p).wait_send()
                back_ring(s + 1, p).wait_send()
            if s < last or not DIAG:
                side(s, p).wait_send()
            if s == last and DIAG:
                diag(p).wait_send()
        if s < last or not DIAG:
            back_side(s).wait_send()
        else:
            back_diag().wait_send()
    store_dq.wait()
    store_dk.wait()
    store_dv.wait()


def per_device(queries, keys, values, out_grad, block_place):
    tokens, size = keys.shape
    heads = queries.shape[1] // size
    own_rows = heads * tokens
    rows = 2 * own_rows
    chunks = 2 * STEPS
    dma = lambda count: pltpu.SemaphoreType.DMA((count,))
    hbm = pl.BlockSpec(memory_space=pl.ANY)
    kept = lambda *shape: pltpu.VMEM(shape, F32)
    low = lambda *shape: pltpu.VMEM(shape, BF16)
    body = functools.partial(
        kernel, lax.axis_size("inner"), lax.axis_size("outer"), tokens, size, heads
    )
    return pl.pallas_call(
        body,
        out_shape=(
            jax.ShapeDtypeStruct(queries.shape, BF16),
            jax.ShapeDtypeStruct(keys.shape, BF16),
            jax.ShapeDtypeStruct(values.shape, BF16),
        ),
        in_specs=[pl.BlockSpec(memory_space=pltpu.SMEM), hbm, hbm, hbm, hbm],
        out_specs=(hbm, hbm, hbm),
        scratch_shapes=[
            low(chunks, 2, tokens, size),
            low(2, tokens, heads * size), low(2, tokens, heads * size), low(size, rows), low(size, rows),
            low(chunks, tokens, rows), kept(chunks, tokens, rows), kept(chunks, 1, rows),
            kept(8, rows), kept(8, rows), kept(size, rows), kept(size, own_rows),
            kept(STEPS, 2, tokens, size),
            low(STEPS, 2, tokens, size), low(STEPS, 2, tokens, size),
            low(STEPS, 2, tokens, size), low(STEPS, 2, tokens, size), low(2, tokens, size),
            low(tokens, heads * size),
            dma(4), dma(3), dma(2), dma(2), dma(2), dma(2), dma(1), dma(1),
            dma(chunks), dma(chunks), dma(chunks), dma(chunks), dma(2), dma(2),
            dma(chunks), dma(chunks), dma(STEPS), dma(STEPS), dma(1), dma(1),
        ],
        compiler_params=pltpu.CompilerParams(
            collective_id=0, has_side_effects=True, vmem_limit_bytes=58 * 2**20
        ),
        cost_estimate=pl.CostEstimate(
            flops=10 * rows * chunks * tokens * size,
            bytes_accessed=6 * tokens * size * (heads + 1),
            transcendentals=rows * chunks * tokens,
        ),
        name="attention_backward",
    )(block_place, queries, keys, values, out_grad)


def solution(mesh):
    placed = P(("inner", "outer"), None)
    return jax.shard_map(
        per_device,
        mesh=mesh,
        in_specs=(placed, placed, placed, placed, P()),
        out_specs=(placed, placed, placed),
        check_vma=False,
    )
```

```python
import functools
import math

import jax
import jax.numpy as jnp
from jax import lax
from jax.experimental import pallas as pl
from jax.experimental.pallas import tpu as pltpu
from jax.sharding import PartitionSpec as P

STEPS = 4
LINE = 8
PIECES = 4
F32, BF16 = jnp.float32, jnp.bfloat16
MESH = pl.DeviceIdType.MESH
LOW = -1e30


def dot(a, b, over=(1, 0)):
    dims = (((over[0],), (over[1],)), ((), ()))
    return lax.dot_general(a, b, dims, preferred_element_type=F32)


def kernel(
    inner_size, outer_size, tokens, size, heads,
    place_ref, q_hbm, k_hbm, v_hbm, g_hbm, dq_ref, dk_ref, dv_ref,
    kv, q_nat, g_nat, q_cols, g_cols, probs, grads, maxes, stats, stats_in, dq_cols, dq_in,
    near, pair_out, pair_in, ring_out, ring_in,
    load_sem, q_s, q_r, stats_s, stats_r, dq_s, dq_r,
    ring_s, ring_r, pair_s, pair_r, back_ring_s, back_ring_r, back_pair_s, back_pair_r,
):
    inner, outer = lax.axis_index("inner"), lax.axis_index("outer")
    core, depth = inner % 2, outer % LINE
    other_core = inner + 1 - 2 * core
    other_pair = (inner + 2) % inner_size
    after_side = (inner + 2 * core * (depth // (LINE - 1))) % inner_size
    before_side = (inner + 2 * core * ((LINE - 1 - depth) // (LINE - 1))) % inner_size
    after = (after_side, (outer + 1) % outer_size)
    before = (before_side, (outer + outer_size - 1) % outer_size)
    mate = (other_core, outer)
    pair = (other_pair, outer)
    own_rows = heads * tokens
    rows = 2 * own_rows
    block = tokens // 2
    scale = 1.0 / math.sqrt(size)
    scale2 = scale * math.log2(math.e)

    loads = [
        pltpu.make_async_copy(src, dst, load_sem.at[n])
        for n, (src, dst) in enumerate(
            ((k_hbm, kv.at[0, 0]), (v_hbm, kv.at[0, 1]), (q_hbm, q_nat.at[0]), (g_hbm, g_nat.at[0]))
        )
    ]
    for load in loads:
        load.start()

    partners = [mate, pair, after, before]
    barrier = pltpu.get_barrier_semaphore()
    for partner in partners:
        pl.semaphore_signal(barrier, inc=1, device_id=partner, device_id_type=MESH)
    pl.semaphore_wait(barrier, len(partners))

    def remote(src, dst, send, recv, to):
        return pltpu.make_async_remote_copy(
            src_ref=src, dst_ref=dst, send_sem=send, recv_sem=recv, device_id=to, device_id_type=MESH
        )

    def piece(ref, p):
        per = PIECES // 2
        length = tokens // per
        return ref.at[p // per, pl.ds((p % per) * length, length)]

    def ring(s, p):
        n = PIECES * s + p
        return remote(piece(kv.at[2 * s], p), piece(kv.at[2 * s + 2], p), ring_s.at[n], ring_r.at[n], after)

    def side(s, p):
        n = PIECES * s + p
        return remote(piece(kv.at[2 * s], p), piece(kv.at[2 * s + 1], p), pair_s.at[n], pair_r.at[n], pair)

    q_over = remote(q_hbm, q_nat.at[1], q_s.at[0], q_r.at[0], mate)
    g_over = remote(g_hbm, g_nat.at[1], q_s.at[1], q_r.at[1], mate)
    loads[0].wait()
    loads[1].wait()
    for p in range(PIECES):
        ring(0, p).start()
    for p in range(PIECES):
        side(0, p).start()
    q_over.start()
    g_over.start()

    lane = lax.broadcasted_iota(jnp.int32, (1, own_rows), 1)

    def row_places(side_inner):
        first_block = 2 * (side_inner * outer_size + outer)
        return jnp.where((lane // block) % 2 == 0, place_ref[first_block], place_ref[first_block + 1])

    q_place = jnp.concatenate([row_places(inner), row_places(other_core)], axis=1)

    def turn(n):
        for h in range(heads):
            there = pl.ds(n * own_rows + h * tokens, tokens)
            q_cols[:, there] = q_nat[n, :, h * size : (h + 1) * size].T
            g_cols[:, there] = g_nat[n, :, h * size : (h + 1) * size].T

    loads[2].wait()
    loads[3].wait()
    turn(0)
    q_over.wait_recv()
    g_over.wait_recv()
    turn(1)

    def key_block(s, j):
        crossed = jnp.where(depth < s, core, 0)
        column = (inner + 2 * crossed + 2 * j) % inner_size
        return 2 * (column * outer_size + (outer + outer_size - s) % outer_size)

    def forward(s, j, first=False):
        c = 2 * s + j
        keys, values = kv[c, 0], kv[c, 1]
        places = [place_ref[key_block(s, j) + b] for b in range(2)]
        for t in range(rows // tokens):
            at = slice(t * tokens, (t + 1) * tokens)
            place = q_place[:, at]
            bias = [jnp.broadcast_to(jnp.where(p <= place, 0.0, LOW).astype(F32), (block, tokens)) for p in places]
            if first and t < heads:
                row = lax.broadcasted_iota(jnp.int32, (block, tokens), 0)
                col = lax.broadcasted_iota(jnp.int32, (block, tokens), 1) % block
                for b in range(2):
                    ok = places[b] * block + row <= place * block + col
                    bias[b] = jnp.where(ok, 0.0, LOW).astype(F32)
            scores = dot(keys, q_cols[:, at]) * scale2 + jnp.concatenate(bias, axis=0)
            grad_probs = dot(values, g_cols[:, at])
            new_max = jnp.max(scores, axis=0, keepdims=True)
            if not first:
                old_max = stats[0:1, at]
                new_max = jnp.maximum(old_max, new_max)
                fade = jnp.exp2(old_max - new_max)
            weights = jnp.exp2(scores - new_max)
            part_sum = jnp.sum(weights, axis=0, keepdims=True)
            part_dot = jnp.sum(weights * grad_probs, axis=0, keepdims=True)
            if not first:
                part_sum += stats[1:2, at] * fade
                part_dot += stats[2:3, at] * fade
            stats[0:1, at] = new_max
            stats[1:2, at] = part_sum
            stats[2:3, at] = part_dot
            probs[c, :, at] = weights.astype(BF16)
            grads[c, :, at] = grad_probs
            maxes[c, :, at] = new_max

    forward(0, 0, first=True)

    def arrive(s, _):
        for p in range(PIECES):
            ring(s - 1, p).wait_recv()

            @pl.when(s < STEPS - 1)
            def _():
                ring(s, p).start()

            side(s, p).start()

        forward(s, 0)
        for p in range(PIECES):
            side(s - 1, p).wait_recv()
        forward(s - 1, 1)
        return 0

    lax.fori_loop(1, STEPS, arrive, 0)
    last = STEPS - 1
    for p in range(PIECES):
        side(last, p).wait_recv()
    forward(last, 1)

    def swap_stats(n):
        here = pl.ds(n * own_rows, own_rows)
        there = pl.ds((1 - n) * own_rows, own_rows)
        return remote(stats.at[:, here], stats_in.at[:, there], stats_s.at[n], stats_r.at[n], mate)

    for n in range(2):
        swap_stats(n).start()
    dq_cols[...] = jnp.zeros_like(dq_cols)
    for n in range(2):
        swap_stats(n).wait()
    top = jnp.maximum(stats[0:1, :], stats_in[0:1, :])
    here, there = jnp.exp2(stats[0:1, :] - top), jnp.exp2(stats_in[0:1, :] - top)
    inverse = 1.0 / (stats[1:2, :] * here + stats_in[1:2, :] * there)
    mean = (stats[2:3, :] * here + stats_in[2:3, :] * there) * inverse
    stats[0:1, :] = top
    stats[1:2, :] = inverse
    stats[2:3, :] = mean

    def backward(c):
        keys = kv[c, 0]
        dk = jnp.zeros((tokens, size), F32)
        dv = jnp.zeros((tokens, size), F32)
        factor = jnp.exp2(maxes[c] - stats[0:1, :]) * stats[1:2, :]
        for t in range(rows // tokens):
            at = slice(t * tokens, (t + 1) * tokens)
            n, h = t // heads, t % heads
            cut = slice(h * size, (h + 1) * size)
            weights = probs[c, :, at].astype(F32) * factor[:, at]
            slopes = (weights * (grads[c, :, at] - stats[2:3, at])).astype(BF16)
            dv += dot(weights.astype(BF16), g_nat[n, :, cut])
            dk += dot(slopes, q_nat[n, :, cut])
            dq_cols[:, at] += dot(keys, slopes, (0, 0))
        return dk * scale, dv

    def back_side(s):
        return remote(pair_out.at[s], pair_in.at[s], back_pair_s.at[s], back_pair_r.at[s], pair)

    def back_ring(s, p):
        n = PIECES * s + p
        return remote(
            piece(ring_out.at[s], p), piece(ring_in.at[s - 1], p), back_ring_s.at[n], back_ring_r.at[n - PIECES], before
        )

    def arrived(s, p):
        n = PIECES * s + p
        return remote(piece(ring_out.at[s], p), piece(ring_in.at[s], p), back_ring_s.at[n], back_ring_r.at[n], before)

    def settle(s):
        back_side(s).wait_recv()
        per = PIECES // 2
        length = tokens // per
        for p in range(PIECES):
            at = (p // per, slice((p % per) * length, (p % per + 1) * length))
            whole = near[(s, *at)] + pair_in[(s, *at)].astype(F32)
            if s < last:
                arrived(s, p).wait_recv()
                whole = whole + ring_in[(s, *at)].astype(F32)
            if s > 0:
                ring_out[(s, *at)] = whole.astype(BF16)
                back_ring(s, p).start()
            else:
                (dk_ref, dv_ref)[at[0]][at[1], :] = whole.astype(BF16)

    def leave(n, _):
        s, j = last - 2 * (n // 4) - n % 2, 1 - (n % 4) // 2
        dk, dv = backward(2 * s + j)

        @pl.when(j == 1)
        def _():
            pair_out[s, 0] = dk.astype(BF16)
            pair_out[s, 1] = dv.astype(BF16)
            back_side(s).start()

        @pl.when(j == 0)
        def _():
            near[s, 0] = dk
            near[s, 1] = dv

        @pl.when(n == 5)
        def _():
            settle(last)

        return 0

    lax.fori_loop(0, 2 * STEPS, leave, 0)

    dq_over = remote(dq_cols.at[:, pl.ds(own_rows, own_rows)], dq_in, dq_s.at[0], dq_r.at[0], mate)
    dq_over.start()
    settle(last - 1)
    dq_over.wait_recv()
    for h in range(heads):
        there = slice(h * tokens, (h + 1) * tokens)
        part = (dq_cols[:, there] + dq_in[:, there]) * scale
        dq_ref[:, h * size : (h + 1) * size] = part.T.astype(BF16)
    for s in reversed(range(last - 1)):
        settle(s)
    q_over.wait_send()
    g_over.wait_send()
    dq_over.wait_send()
    for s in range(STEPS):
        for p in range(PIECES):
            if s < last:
                ring(s, p).wait_send()
                back_ring(s + 1, p).wait_send()
            side(s, p).wait_send()
        back_side(s).wait_send()


def store(*refs):
    sem, count = refs[-1], len(refs) // 2
    copies = [pltpu.make_async_copy(refs[n], refs[count + n], sem.at[n]) for n in range(count)]
    for copy in copies:
        copy.start()
    for copy in copies:
        copy.wait()


def per_device(queries, keys, values, out_grad, block_place):
    tokens, size = keys.shape
    heads = queries.shape[1] // size
    own_rows = heads * tokens
    rows = 2 * own_rows
    chunks = 2 * STEPS
    dma = lambda count: pltpu.SemaphoreType.DMA((count,))
    hbm = pl.BlockSpec(memory_space=pl.ANY)
    kept = lambda *shape: pltpu.VMEM(shape, F32)
    low = lambda *shape: pltpu.VMEM(shape, BF16)
    body = functools.partial(
        kernel, lax.axis_size("inner"), lax.axis_size("outer"), tokens, size, heads
    )
    results = pl.pallas_call(
        body,
        out_shape=(
            pltpu.VMEM(queries.shape, BF16),
            pltpu.VMEM(keys.shape, BF16),
            pltpu.VMEM(values.shape, BF16),
        ),
        in_specs=[pl.BlockSpec(memory_space=pltpu.SMEM), hbm, hbm, hbm, hbm],
        out_specs=(pl.BlockSpec(memory_space=pltpu.VMEM),) * 3,
        scratch_shapes=[
            low(chunks, 2, tokens, size),
            low(2, tokens, heads * size), low(2, tokens, heads * size), low(size, rows), low(size, rows),
            low(chunks, tokens, rows), kept(chunks, tokens, rows), kept(chunks, 1, rows),
            kept(8, rows), kept(8, rows), kept(size, rows), kept(size, own_rows),
            kept(STEPS, 2, tokens, size),
            low(STEPS, 2, tokens, size), low(STEPS, 2, tokens, size),
            low(STEPS, 2, tokens, size), low(STEPS, 2, tokens, size),
            dma(4), dma(2), dma(2), dma(2), dma(2), dma(1), dma(1),
            *[dma(PIECES * STEPS)] * 6, dma(STEPS), dma(STEPS),
        ],
        compiler_params=pltpu.CompilerParams(
            collective_id=0, has_side_effects=True, vmem_limit_bytes=58 * 2**20
        ),
        cost_estimate=pl.CostEstimate(
            flops=10 * rows * chunks * tokens * size,
            bytes_accessed=6 * tokens * size * (heads + 1),
            transcendentals=rows * chunks * tokens,
        ),
        name="attention_backward",
    )(block_place, queries, keys, values, out_grad)
    shapes = tuple(jax.ShapeDtypeStruct(r.shape, r.dtype) for r in results)
    return pl.pallas_call(
        store,
        out_shape=shapes,
        in_specs=[pl.BlockSpec(memory_space=pltpu.VMEM)] * len(shapes),
        out_specs=(hbm,) * len(shapes),
        scratch_shapes=[dma(len(shapes))],
        name="store_gradients",
    )(*(pltpu.with_memory_space_constraint(r, pltpu.VMEM) for r in results))


def solution(mesh):
    placed = P(("inner", "outer"), None)
    return jax.shard_map(
        per_device,
        mesh=mesh,
        in_specs=(placed, placed, placed, placed, P()),
        out_specs=(placed, placed, placed),
        check_vma=False,
    )
```

```python
import functools
import math

import jax
import jax.numpy as jnp
from jax import lax
from jax.experimental import pallas as pl
from jax.experimental.pallas import tpu as pltpu
from jax.sharding import PartitionSpec as P

STEPS = 4
LINE = 8
PIECES = 4
F32, BF16 = jnp.float32, jnp.bfloat16
MESH = pl.DeviceIdType.MESH
LOW = -1e30


def dot(a, b, over=(1, 0)):
    dims = (((over[0],), (over[1],)), ((), ()))
    return lax.dot_general(a, b, dims, preferred_element_type=F32)


def kernel(
    inner_size, outer_size, tokens, size, heads,
    place_ref, q_hbm, k_hbm, v_hbm, g_hbm, dq_ref, dk_ref, dv_ref,
    kv, q_nat, g_nat, q_cols, g_cols, probs, grads, maxes, stats, stats_in, dq_cols, dq_in,
    near, pair_out, pair_in, ring_out, ring_in,
    load_sem, q_s, q_r, stats_s, stats_r, dq_s, dq_r,
    ring_s, ring_r, pair_s, pair_r, back_ring_s, back_ring_r, back_pair_s, back_pair_r,
):
    inner, outer = lax.axis_index("inner"), lax.axis_index("outer")
    core, depth = inner % 2, outer % LINE
    other_core = inner + 1 - 2 * core
    other_pair = (inner + 2) % inner_size
    after_side = (inner + 2 * core * (depth // (LINE - 1))) % inner_size
    before_side = (inner + 2 * core * ((LINE - 1 - depth) // (LINE - 1))) % inner_size
    after = (after_side, (outer + 1) % outer_size)
    before = (before_side, (outer + outer_size - 1) % outer_size)
    mate = (other_core, outer)
    pair = (other_pair, outer)
    own_rows = heads * tokens
    rows = 2 * own_rows
    block = tokens // 2
    scale = 1.0 / math.sqrt(size)
    scale2 = scale * math.log2(math.e)

    loads = [
        pltpu.make_async_copy(src, dst, load_sem.at[n])
        for n, (src, dst) in enumerate(
            ((k_hbm, kv.at[0, 0]), (v_hbm, kv.at[0, 1]), (q_hbm, q_nat.at[core]), (g_hbm, g_nat.at[core]))
        )
    ]
    for load in loads:
        load.start()

    partners = [mate, pair, after, before]
    barrier = pltpu.get_barrier_semaphore()
    for partner in partners:
        pl.semaphore_signal(barrier, inc=1, device_id=partner, device_id_type=MESH)
    pl.semaphore_wait(barrier, len(partners))

    def remote(src, dst, send, recv, to):
        return pltpu.make_async_remote_copy(
            src_ref=src, dst_ref=dst, send_sem=send, recv_sem=recv, device_id=to, device_id_type=MESH
        )

    def piece(ref, p):
        per = PIECES // 2
        length = tokens // per
        return ref.at[p // per, pl.ds((p % per) * length, length)]

    def ring(s, p):
        n = PIECES * s + p
        return remote(piece(kv.at[2 * s], p), piece(kv.at[2 * s + 2], p), ring_s.at[n], ring_r.at[n], after)

    def side(s, p):
        n = PIECES * s + p
        return remote(piece(kv.at[2 * s], p), piece(kv.at[2 * s + 1], p), pair_s.at[n], pair_r.at[n], pair)

    q_over = remote(q_hbm, q_nat.at[core], q_s.at[0], q_r.at[0], mate)
    g_over = remote(g_hbm, g_nat.at[core], q_s.at[1], q_r.at[1], mate)
    loads[0].wait()
    loads[1].wait()
    for p in range(PIECES):
        ring(0, p).start()
    for p in range(PIECES):
        side(0, p).start()
    q_over.start()
    g_over.start()

    lane = lax.broadcasted_iota(jnp.int32, (1, own_rows), 1)

    def row_places(side_inner):
        first_block = 2 * (side_inner * outer_size + outer)
        return jnp.where((lane // block) % 2 == 0, place_ref[first_block], place_ref[first_block + 1])

    q_place = jnp.concatenate([row_places(inner - core), row_places(inner - core + 1)], axis=1)

    def turn(n):
        for h in range(heads):
            there = pl.ds(pl.multiple_of(n * own_rows + h * tokens, tokens), tokens)
            q_cols[:, there] = q_nat[n, :, h * size : (h + 1) * size].T
            g_cols[:, there] = g_nat[n, :, h * size : (h + 1) * size].T

    loads[2].wait()
    loads[3].wait()
    turn(core)
    q_over.wait_recv()
    g_over.wait_recv()
    turn(1 - core)

    def key_block(s, j):
        crossed = jnp.where(depth < s, core, 0)
        column = (inner + 2 * crossed + 2 * j) % inner_size
        return 2 * (column * outer_size + (outer + outer_size - s) % outer_size)

    def forward(s, j, first=False, tiles=range(rows // tokens)):
        c = 2 * s + j
        keys, values = kv[c, 0], kv[c, 1]
        places = [place_ref[key_block(s, j) + b] for b in range(2)]
        for t in tiles:
            at = slice(t * tokens, (t + 1) * tokens)
            place = q_place[:, at]
            bias = [jnp.broadcast_to(jnp.where(p <= place, 0.0, LOW).astype(F32), (block, tokens)) for p in places]
            if first:
                row = lax.broadcasted_iota(jnp.int32, (block, tokens), 0)
                col = lax.broadcasted_iota(jnp.int32, (block, tokens), 1) % block
                for b in range(2):
                    ok = places[b] * block + row <= place * block + col
                    bias[b] = jnp.where(ok, 0.0, LOW).astype(F32)
            scores = dot(keys, q_cols[:, at]) * scale2 + jnp.concatenate(bias, axis=0)
            grad_probs = dot(values, g_cols[:, at])
            new_max = jnp.max(scores, axis=0, keepdims=True)
            if not first:
                old_max = stats[0:1, at]
                new_max = jnp.maximum(old_max, new_max)
                fade = jnp.exp2(old_max - new_max)
            weights = jnp.exp2(scores - new_max)
            part_sum = jnp.sum(weights, axis=0, keepdims=True)
            part_dot = jnp.sum(weights * grad_probs, axis=0, keepdims=True)
            if not first:
                part_sum += stats[1:2, at] * fade
                part_dot += stats[2:3, at] * fade
            stats[0:1, at] = new_max
            stats[1:2, at] = part_sum
            stats[2:3, at] = part_dot
            probs[c, :, at] = weights.astype(BF16)
            grads[c, :, at] = grad_probs
            maxes[c, :, at] = new_max

    forward(0, 0, first=True)

    def arrive(s, _):
        for p in range(PIECES):
            ring(s - 1, p).wait_recv()

            @pl.when(s < STEPS - 1)
            def _():
                ring(s, p).start()

            side(s, p).start()

        forward(s, 0)
        for p in range(PIECES):
            side(s - 1, p).wait_recv()
        forward(s - 1, 1)
        return 0

    lax.fori_loop(1, STEPS, arrive, 0)
    last = STEPS - 1
    for p in range(PIECES):
        side(last, p).wait_recv()
    dq_cols[...] = jnp.zeros_like(dq_cols)

    def join(n):
        at = pl.ds(n * own_rows, own_rows)
        return remote(stats.at[:, at], stats_in.at[:, at], stats_s.at[n], stats_r.at[n], mate)

    def joined(n):
        join(n).wait()
        at = slice(n * own_rows, (n + 1) * own_rows)
        top = jnp.maximum(stats[0:1, at], stats_in[0:1, at])
        here, there = jnp.exp2(stats[0:1, at] - top), jnp.exp2(stats_in[0:1, at] - top)
        inverse = 1.0 / (stats[1:2, at] * here + stats_in[1:2, at] * there)
        mean = (stats[2:3, at] * here + stats_in[2:3, at] * there) * inverse
        stats[0:1, at] = top
        stats[1:2, at] = inverse
        stats[2:3, at] = mean

    halves = [range(n * heads, (n + 1) * heads) for n in range(2)]
    for n in range(2):
        forward(last, 1, tiles=halves[n])
        join(n).start()

    def backward(c, tiles=range(rows // tokens), dk=None, dv=None):
        keys = kv[c, 0]
        dk = jnp.zeros((tokens, size), F32) if dk is None else dk
        dv = jnp.zeros((tokens, size), F32) if dv is None else dv
        for t in tiles:
            at = slice(t * tokens, (t + 1) * tokens)
            n, h = t // heads, t % heads
            cut = slice(h * size, (h + 1) * size)
            factor = jnp.exp2(maxes[c, :, at] - stats[0:1, at]) * stats[1:2, at]
            weights = probs[c, :, at].astype(F32) * factor
            slopes = (weights * (grads[c, :, at] - stats[2:3, at])).astype(BF16)
            dv += dot(weights.astype(BF16), g_nat[n, :, cut])
            dk += dot(slopes, q_nat[n, :, cut])
            dq_cols[:, at] += dot(keys, slopes, (0, 0))
        return dk, dv

    def back_side(s):
        return remote(pair_out.at[s], pair_in.at[s], back_pair_s.at[s], back_pair_r.at[s], pair)

    def back_ring(s, p):
        n = PIECES * s + p
        return remote(
            piece(ring_out.at[s], p), piece(ring_in.at[s - 1], p), back_ring_s.at[n], back_ring_r.at[n - PIECES], before
        )

    def arrived(s, p):
        n = PIECES * s + p
        return remote(piece(ring_out.at[s], p), piece(ring_in.at[s], p), back_ring_s.at[n], back_ring_r.at[n], before)

    def settle(s):
        back_side(s).wait_recv()
        per = PIECES // 2
        length = tokens // per
        for p in range(PIECES):
            at = (p // per, slice((p % per) * length, (p % per + 1) * length))
            whole = near[(s, *at)] + pair_in[(s, *at)].astype(F32)
            if s < last:
                arrived(s, p).wait_recv()
                whole = whole + ring_in[(s, *at)].astype(F32)
            if s > 0:
                ring_out[(s, *at)] = whole.astype(BF16)
                back_ring(s, p).start()
            else:
                (dk_ref, dv_ref)[at[0]][at[1], :] = whole.astype(BF16)

    joined(0)
    dk, dv = backward(2 * last + 1, halves[0])
    joined(1)
    dk, dv = backward(2 * last + 1, halves[1], dk, dv)
    pair_out[last, 0] = (dk * scale).astype(BF16)
    pair_out[last, 1] = dv.astype(BF16)
    back_side(last).start()

    def leave(n, _):
        s, j = last - n // 2, 1 - n % 2
        dk, dv = backward(2 * s + j)
        dk = dk * scale

        @pl.when(j == 1)
        def _():
            pair_out[s, 0] = dk.astype(BF16)
            pair_out[s, 1] = dv.astype(BF16)
            back_side(s).start()

        @pl.when(j == 0)
        def _():
            near[s, 0] = dk
            near[s, 1] = dv

        @pl.when(n == 4)
        def _():
            settle(last)

        return 0

    lax.fori_loop(1, 2 * STEPS, leave, 0)

    dq_over = remote(dq_cols.at[:, pl.ds(pl.multiple_of((1 - core) * own_rows, own_rows), own_rows)], dq_in, dq_s.at[0], dq_r.at[0], mate)
    dq_over.start()
    settle(last - 1)
    dq_over.wait_recv()
    for h in range(heads):
        here = pl.ds(pl.multiple_of(core * own_rows + h * tokens, tokens), tokens)
        part = (dq_cols[:, here] + dq_in[:, h * tokens : (h + 1) * tokens]) * scale
        dq_ref[:, h * size : (h + 1) * size] = part.T.astype(BF16)
    for s in reversed(range(last - 1)):
        settle(s)
    q_over.wait_send()
    g_over.wait_send()
    dq_over.wait_send()
    for s in range(STEPS):
        for p in range(PIECES):
            if s < last:
                ring(s, p).wait_send()
                back_ring(s + 1, p).wait_send()
            side(s, p).wait_send()
        back_side(s).wait_send()


def store(*refs):
    sem, count = refs[-1], len(refs) // 2
    copies = [pltpu.make_async_copy(refs[n], refs[count + n], sem.at[n]) for n in range(count)]
    for copy in copies:
        copy.start()
    for copy in copies:
        copy.wait()


def per_device(queries, keys, values, out_grad, block_place):
    tokens, size = keys.shape
    heads = queries.shape[1] // size
    own_rows = heads * tokens
    rows = 2 * own_rows
    chunks = 2 * STEPS
    dma = lambda count: pltpu.SemaphoreType.DMA((count,))
    hbm = pl.BlockSpec(memory_space=pl.ANY)
    kept = lambda *shape: pltpu.VMEM(shape, F32)
    low = lambda *shape: pltpu.VMEM(shape, BF16)
    body = functools.partial(
        kernel, lax.axis_size("inner"), lax.axis_size("outer"), tokens, size, heads
    )
    results = pl.pallas_call(
        body,
        out_shape=(
            pltpu.VMEM(queries.shape, BF16),
            pltpu.VMEM(keys.shape, BF16),
            pltpu.VMEM(values.shape, BF16),
        ),
        in_specs=[pl.BlockSpec(memory_space=pltpu.SMEM), hbm, hbm, hbm, hbm],
        out_specs=(pl.BlockSpec(memory_space=pltpu.VMEM),) * 3,
        scratch_shapes=[
            low(chunks, 2, tokens, size),
            low(2, tokens, heads * size), low(2, tokens, heads * size), low(size, rows), low(size, rows),
            low(chunks, tokens, rows), kept(chunks, tokens, rows), kept(chunks, 1, rows),
            kept(8, rows), kept(8, rows), kept(size, rows), kept(size, own_rows),
            kept(STEPS, 2, tokens, size),
            low(STEPS, 2, tokens, size), low(STEPS, 2, tokens, size),
            low(STEPS, 2, tokens, size), low(STEPS, 2, tokens, size),
            dma(4), dma(2), dma(2), dma(2), dma(2), dma(1), dma(1),
            *[dma(PIECES * STEPS)] * 6, dma(STEPS), dma(STEPS),
        ],
        compiler_params=pltpu.CompilerParams(
            collective_id=0, has_side_effects=True, vmem_limit_bytes=58 * 2**20
        ),
        cost_estimate=pl.CostEstimate(
            flops=10 * rows * chunks * tokens * size,
            bytes_accessed=6 * tokens * size * (heads + 1),
            transcendentals=rows * chunks * tokens,
        ),
        name="attention_backward",
    )(block_place, queries, keys, values, out_grad)
    shapes = tuple(jax.ShapeDtypeStruct(r.shape, r.dtype) for r in results)
    return pl.pallas_call(
        store,
        out_shape=shapes,
        in_specs=[pl.BlockSpec(memory_space=pltpu.VMEM)] * len(shapes),
        out_specs=(hbm,) * len(shapes),
        scratch_shapes=[dma(len(shapes))],
        name="store_gradients",
    )(*(pltpu.with_memory_space_constraint(r, pltpu.VMEM) for r in results))


def solution(mesh):
    placed = P(("inner", "outer"), None)
    return jax.shard_map(
        per_device,
        mesh=mesh,
        in_specs=(placed, placed, placed, placed, P()),
        out_specs=(placed, placed, placed),
        check_vma=False,
    )
```

```python
import functools
import math

import jax
import jax.numpy as jnp
from jax import lax
from jax.experimental import pallas as pl
from jax.experimental.pallas import tpu as pltpu
from jax.sharding import PartitionSpec as P

STEPS = 4
LINE = 8
PIECES = 4
F32, BF16 = jnp.float32, jnp.bfloat16
MESH = pl.DeviceIdType.MESH
LOW = -1e30


def dot(a, b, over=(1, 0)):
    dims = (((over[0],), (over[1],)), ((), ()))
    return lax.dot_general(a, b, dims, preferred_element_type=F32)


def kernel(
    inner_size, outer_size, tokens, size, heads,
    place_ref, q_hbm, k_hbm, v_hbm, g_hbm, dq_ref, dk_ref, dv_ref,
    kv, q_nat, g_nat, q_cols, g_cols, probs, grads, maxes, stats, stats_in, dq_cols, dq_in,
    near, pair_out, pair_in, ring_out, ring_in,
    load_sem, q_s, q_r, stats_s, stats_r, dq_s, dq_r,
    ring_s, ring_r, pair_s, pair_r, back_ring_s, back_ring_r, back_pair_s, back_pair_r,
):
    inner, outer = lax.axis_index("inner"), lax.axis_index("outer")
    core, depth = inner % 2, outer % LINE
    other_core = inner + 1 - 2 * core
    other_pair = (inner + 2) % inner_size
    after_side = (inner + 2 * core * (depth // (LINE - 1))) % inner_size
    before_side = (inner + 2 * core * ((LINE - 1 - depth) // (LINE - 1))) % inner_size
    after = (after_side, (outer + 1) % outer_size)
    before = (before_side, (outer + outer_size - 1) % outer_size)
    mate = (other_core, outer)
    pair = (other_pair, outer)
    own_rows = heads * tokens
    rows = 2 * own_rows
    block = tokens // 2
    scale = 1.0 / math.sqrt(size)
    scale2 = scale * math.log2(math.e)

    loads = [
        pltpu.make_async_copy(src, dst, load_sem.at[n])
        for n, (src, dst) in enumerate(
            ((k_hbm, kv.at[0, 0]), (v_hbm, kv.at[0, 1]), (q_hbm, q_nat.at[core]), (g_hbm, g_nat.at[core]))
        )
    ]
    for load in loads:
        load.start()

    partners = [mate, pair, after, before]
    barrier = pltpu.get_barrier_semaphore()
    for partner in partners:
        pl.semaphore_signal(barrier, inc=1, device_id=partner, device_id_type=MESH)
    pl.semaphore_wait(barrier, len(partners))

    def remote(src, dst, send, recv, to):
        return pltpu.make_async_remote_copy(
            src_ref=src, dst_ref=dst, send_sem=send, recv_sem=recv, device_id=to, device_id_type=MESH
        )

    def piece(ref, p):
        per = PIECES // 2
        length = tokens // per
        return ref.at[p // per, pl.ds((p % per) * length, length)]

    def ring(s, p):
        n = PIECES * s + p
        return remote(piece(kv.at[2 * s], p), piece(kv.at[2 * s + 2], p), ring_s.at[n], ring_r.at[n], after)

    def side(s, p):
        n = PIECES * s + p
        return remote(piece(kv.at[2 * s], p), piece(kv.at[2 * s + 1], p), pair_s.at[n], pair_r.at[n], pair)

    q_over = remote(q_hbm, q_nat.at[core], q_s.at[0], q_r.at[0], mate)
    g_over = remote(g_hbm, g_nat.at[core], q_s.at[1], q_r.at[1], mate)
    loads[0].wait()
    loads[1].wait()
    for p in range(PIECES):
        ring(0, p).start()
    for p in range(PIECES):
        side(0, p).start()
    q_over.start()
    g_over.start()

    lane = lax.broadcasted_iota(jnp.int32, (1, own_rows), 1)

    def row_places(side_inner):
        first_block = 2 * (side_inner * outer_size + outer)
        return jnp.where((lane // block) % 2 == 0, place_ref[first_block], place_ref[first_block + 1])

    q_place = jnp.concatenate([row_places(inner - core), row_places(inner - core + 1)], axis=1)

    def turn(n):
        for h in range(heads):
            there = pl.ds(pl.multiple_of(n * own_rows + h * tokens, tokens), tokens)
            q_cols[:, there] = q_nat[n, :, h * size : (h + 1) * size].T
            g_cols[:, there] = g_nat[n, :, h * size : (h + 1) * size].T

    loads[2].wait()
    loads[3].wait()
    turn(core)
    q_over.wait_recv()
    g_over.wait_recv()
    turn(1 - core)

    def key_block(s, j):
        crossed = jnp.where(depth < s, core, 0)
        column = (inner + 2 * crossed + 2 * j) % inner_size
        return 2 * (column * outer_size + (outer + outer_size - s) % outer_size)

    def forward(s, j, first=False, tiles=range(rows // tokens)):
        c = 2 * s + j
        keys, values = kv[c, 0], kv[c, 1]
        places = [place_ref[key_block(s, j) + b] for b in range(2)]
        for t in tiles:
            at = slice(t * tokens, (t + 1) * tokens)
            place = q_place[:, at]
            bias = [jnp.broadcast_to(jnp.where(p <= place, 0.0, LOW).astype(F32), (block, tokens)) for p in places]
            if first:
                row = lax.broadcasted_iota(jnp.int32, (block, tokens), 0)
                col = lax.broadcasted_iota(jnp.int32, (block, tokens), 1) % block
                for b in range(2):
                    ok = places[b] * block + row <= place * block + col
                    bias[b] = jnp.where(ok, 0.0, LOW).astype(F32)
            scores = dot(keys, q_cols[:, at]) * scale2 + jnp.concatenate(bias, axis=0)
            grad_probs = dot(values, g_cols[:, at])
            new_max = jnp.max(scores, axis=0, keepdims=True)
            if not first:
                old_max = stats[0:1, at]
                new_max = jnp.maximum(old_max, new_max)
                fade = jnp.exp2(old_max - new_max)
            weights = jnp.exp2(scores - new_max)
            part_sum = jnp.sum(weights, axis=0, keepdims=True)
            part_dot = jnp.sum(weights * grad_probs, axis=0, keepdims=True)
            if not first:
                part_sum += stats[1:2, at] * fade
                part_dot += stats[2:3, at] * fade
            stats[0:1, at] = new_max
            stats[1:2, at] = part_sum
            stats[2:3, at] = part_dot
            probs[c, :, at] = weights.astype(BF16)
            grads[c, :, at] = grad_probs
            maxes[c, :, at] = new_max

    forward(0, 0, first=True)

    def arrive(s, _):
        for p in range(PIECES):
            ring(s - 1, p).wait_recv()

            @pl.when(s < STEPS - 1)
            def _():
                ring(s, p).start()

            side(s, p).start()

        forward(s, 0)
        for p in range(PIECES):
            side(s - 1, p).wait_recv()
        forward(s - 1, 1)
        return 0

    lax.fori_loop(1, STEPS, arrive, 0)
    last = STEPS - 1
    for p in range(PIECES):
        side(last, p).wait_recv()
    dq_cols[...] = jnp.zeros_like(dq_cols)

    def join(n):
        at = pl.ds(n * own_rows, own_rows)
        return remote(stats.at[:, at], stats_in.at[:, at], stats_s.at[n], stats_r.at[n], mate)

    def joined(n):
        join(n).wait()
        at = slice(n * own_rows, (n + 1) * own_rows)
        top = jnp.maximum(stats[0:1, at], stats_in[0:1, at])
        here, there = jnp.exp2(stats[0:1, at] - top), jnp.exp2(stats_in[0:1, at] - top)
        inverse = 1.0 / (stats[1:2, at] * here + stats_in[1:2, at] * there)
        mean = (stats[2:3, at] * here + stats_in[2:3, at] * there) * inverse
        stats[0:1, at] = top
        stats[1:2, at] = inverse
        stats[2:3, at] = mean

    halves = [range(n * heads, (n + 1) * heads) for n in range(2)]
    for n in range(2):
        forward(last, 1, tiles=halves[n])
        join(n).start()

    def backward(c, tiles=range(rows // tokens), dk=None, dv=None):
        keys = kv[c, 0]
        dk = jnp.zeros((tokens, size), F32) if dk is None else dk
        dv = jnp.zeros((tokens, size), F32) if dv is None else dv
        for t in tiles:
            at = slice(t * tokens, (t + 1) * tokens)
            n, h = t // heads, t % heads
            cut = slice(h * size, (h + 1) * size)
            factor = jnp.exp2(maxes[c, :, at] - stats[0:1, at]) * stats[1:2, at]
            weights = probs[c, :, at].astype(F32) * factor
            slopes = (weights * (grads[c, :, at] - stats[2:3, at])).astype(BF16)
            dv += dot(weights.astype(BF16), g_nat[n, :, cut])
            dk += dot(slopes, q_nat[n, :, cut])
            dq_cols[:, at] += dot(keys, slopes, (0, 0))
        return dk, dv

    def back_side(s):
        return remote(pair_out.at[s], pair_in.at[s], back_pair_s.at[s], back_pair_r.at[s], pair)

    def back_ring(s, p):
        n = PIECES * s + p
        return remote(
            piece(ring_out.at[s], p), piece(ring_in.at[s - 1], p), back_ring_s.at[n], back_ring_r.at[n - PIECES], before
        )

    def arrived(s, p):
        n = PIECES * s + p
        return remote(piece(ring_out.at[s], p), piece(ring_in.at[s], p), back_ring_s.at[n], back_ring_r.at[n], before)

    def settle(s):
        back_side(s).wait_recv()
        per = PIECES // 2
        length = tokens // per
        for p in range(PIECES):
            at = (p // per, slice((p % per) * length, (p % per + 1) * length))
            whole = near[(s, *at)] + pair_in[(s, *at)].astype(F32)
            if s < last:
                arrived(s, p).wait_recv()
                whole = whole + ring_in[(s, *at)].astype(F32)
            if s > 0:
                ring_out[(s, *at)] = whole.astype(BF16)
                back_ring(s, p).start()
            else:
                (dk_ref, dv_ref)[at[0]][at[1], :] = whole.astype(BF16)

    joined(0)
    dk, dv = backward(2 * last + 1, halves[0])
    joined(1)
    dk, dv = backward(2 * last + 1, halves[1], dk, dv)
    pair_out[last, 0] = (dk * scale).astype(BF16)
    pair_out[last, 1] = dv.astype(BF16)
    back_side(last).start()

    def leave(n, _):
        s, j = last - n // 2, 1 - n % 2
        dk, dv = backward(2 * s + j)
        dk = dk * scale

        @pl.when(j == 1)
        def _():
            pair_out[s, 0] = dk.astype(BF16)
            pair_out[s, 1] = dv.astype(BF16)
            back_side(s).start()

        @pl.when(j == 0)
        def _():
            near[s, 0] = dk
            near[s, 1] = dv

        @pl.when(n == 4)
        def _():
            settle(last)

        return 0

    lax.fori_loop(1, 2 * STEPS, leave, 0)

    dq_over = remote(dq_cols.at[:, pl.ds(pl.multiple_of((1 - core) * own_rows, own_rows), own_rows)], dq_in, dq_s.at[0], dq_r.at[0], mate)
    dq_over.start()
    settle(last - 1)
    settle(1)
    dq_over.wait_recv()
    for h in range(heads):
        here = pl.ds(pl.multiple_of(core * own_rows + h * tokens, tokens), tokens)
        part = (dq_cols[:, here] + dq_in[:, h * tokens : (h + 1) * tokens]) * scale
        dq_ref[:, h * size : (h + 1) * size] = part.T.astype(BF16)
    settle(0)
    q_over.wait_send()
    g_over.wait_send()
    dq_over.wait_send()
    for s in range(STEPS):
        for p in range(PIECES):
            if s < last:
                ring(s, p).wait_send()
                back_ring(s + 1, p).wait_send()
            side(s, p).wait_send()
        back_side(s).wait_send()


def store(*refs):
    sem, count = refs[-1], len(refs) // 2
    copies = [pltpu.make_async_copy(refs[n], refs[count + n], sem.at[n]) for n in range(count)]
    for copy in copies:
        copy.start()
    for copy in copies:
        copy.wait()


def per_device(queries, keys, values, out_grad, block_place):
    tokens, size = keys.shape
    heads = queries.shape[1] // size
    own_rows = heads * tokens
    rows = 2 * own_rows
    chunks = 2 * STEPS
    dma = lambda count: pltpu.SemaphoreType.DMA((count,))
    hbm = pl.BlockSpec(memory_space=pl.ANY)
    kept = lambda *shape: pltpu.VMEM(shape, F32)
    low = lambda *shape: pltpu.VMEM(shape, BF16)
    body = functools.partial(
        kernel, lax.axis_size("inner"), lax.axis_size("outer"), tokens, size, heads
    )
    results = pl.pallas_call(
        body,
        out_shape=(
            pltpu.VMEM(queries.shape, BF16),
            pltpu.VMEM(keys.shape, BF16),
            pltpu.VMEM(values.shape, BF16),
        ),
        in_specs=[pl.BlockSpec(memory_space=pltpu.SMEM), hbm, hbm, hbm, hbm],
        out_specs=(pl.BlockSpec(memory_space=pltpu.VMEM),) * 3,
        scratch_shapes=[
            low(chunks, 2, tokens, size),
            low(2, tokens, heads * size), low(2, tokens, heads * size), low(size, rows), low(size, rows),
            low(chunks, tokens, rows), kept(chunks, tokens, rows), kept(chunks, 1, rows),
            kept(8, rows), kept(8, rows), kept(size, rows), kept(size, own_rows),
            kept(STEPS, 2, tokens, size),
            low(STEPS, 2, tokens, size), low(STEPS, 2, tokens, size),
            low(STEPS, 2, tokens, size), low(STEPS, 2, tokens, size),
            dma(4), dma(2), dma(2), dma(2), dma(2), dma(1), dma(1),
            *[dma(PIECES * STEPS)] * 6, dma(STEPS), dma(STEPS),
        ],
        compiler_params=pltpu.CompilerParams(
            collective_id=0, has_side_effects=True, vmem_limit_bytes=58 * 2**20
        ),
        cost_estimate=pl.CostEstimate(
            flops=10 * rows * chunks * tokens * size,
            bytes_accessed=6 * tokens * size * (heads + 1),
            transcendentals=rows * chunks * tokens,
        ),
        name="attention_backward",
    )(block_place, queries, keys, values, out_grad)
    shapes = tuple(jax.ShapeDtypeStruct(r.shape, r.dtype) for r in results)
    return pl.pallas_call(
        store,
        out_shape=shapes,
        in_specs=[pl.BlockSpec(memory_space=pltpu.VMEM)] * len(shapes),
        out_specs=(hbm,) * len(shapes),
        scratch_shapes=[dma(len(shapes))],
        name="store_gradients",
    )(*(pltpu.with_memory_space_constraint(r, pltpu.VMEM) for r in results))


def solution(mesh):
    placed = P(("inner", "outer"), None)
    return jax.shard_map(
        per_device,
        mesh=mesh,
        in_specs=(placed, placed, placed, placed, P()),
        out_specs=(placed, placed, placed),
        check_vma=False,
    )
```
